768 devices in a mesh: region: 768 (over x, z, y, core).
Axes of the slice: x: 4, y: 8, z: 12, core: 2. Of those that a mesh axis runs over, the one named last changes fastest.
Arguments:
- right_side: float32 [393216, 512], P('region'), may hold values from -6 to 6
- smoother: float32 [3072, 128, 128], P('region')
- diagonal_blocks: float32 [3072, 128, 128], P('region')
- couplings: float32 [3072, 128, 128], P('region'), may hold values from -0.5 to 0.5
- grad_blocks: float32 [3072, 2, 128, 128], P('region'), may hold values from -0.5 to 0.5
- grad_pattern: int32 [3072, 2], P('region'), may hold values from 0 to 1
- interp_blocks: float32 [3072, 2, 128, 128], P('region'), may hold values from -0.5 to 0.5
- interp_pattern: int32 [3072, 2], P('region'), may hold values from 0 to 3
- node_smoother: float32 [768, 128, 128], P('region')
- vector_smoother: float32 [2304, 128, 128], P('region')
- node_aggregates: int32 [98304], P('region'), may hold values from 0 to 15
- vector_aggregates: int32 [294912], P('region'), may hold values from 0 to 47
- node_coarse: float32 [98304, 128], P('region')
- vector_coarse: float32 [98304, 128], P('region')
Outputs:
- correction: float32 [393216, 512], P('region')
The draws below stay inside these ranges and needn't reach their ends.
Inputs may be any that keep to these rules, and one draw needn't show every extreme that they name: `grad_pattern`: value 1 names the first node block of the next region. `interp_pattern`: value 3 names the first vector-nodal block of the next region.
All inputs are finite; a program needn't handle non-finite values.
Results may differ from the reference program's by a relative error of at most 0.0003.
Values sent between devices are 32-bit elements; how exact they have to be, the bound alone decides.
No kernel may reach another device: no remote copies, remote signals or barrier semaphores. Data moves between devices by JAX's collectives and lax.ppermute only.
A program may use at most 32 MiB of HBM per device.

```python
import math
import jax
import jax.numpy as jnp
from jax import lax

B = 128
R = 512
NB = 4
NN = 1
NV = 3
EDGE_BLOCKS = 3072
EDGES = 393216
NODE_BLOCKS = 768
VEC_BLOCKS = 2304
NODES = 98304
VEC_DOFS = 294912
COARSE = 98304
N_REGION = 768


def dominant(key, amount, diagonal, spread):
    key_rows, key_noise = jax.random.split(key)
    row_scale = jax.random.uniform(key_rows, (amount, B, 1), jnp.float32, 0.6, 1.6)
    jitter = jax.random.normal(key_noise, (amount, B, B), jnp.float32) * (spread / math.sqrt(B))
    return jnp.eye(B, dtype=jnp.float32)[None] * row_scale * diagonal + jitter


def draw_smoother(key, part):
    key = jax.random.fold_in(key, 11)
    return dominant(key, EDGE_BLOCKS, 0.4, 0.15)


def draw_diagonal_blocks(key, part):
    key = jax.random.fold_in(key, 12)
    return dominant(key, EDGE_BLOCKS, 2.0, 0.6)


def draw_node_smoother(key, part):
    key = jax.random.fold_in(key, 13)
    return dominant(key, NODE_BLOCKS, 0.5, 0.2)


def draw_vector_smoother(key, part):
    key = jax.random.fold_in(key, 14)
    return dominant(key, VEC_BLOCKS, 0.5, 0.2)


def draw_node_coarse(key, part):
    key = jax.random.fold_in(key, 15)
    return dominant(key, COARSE // B, 0.3, 0.1).reshape(COARSE, B)


def draw_vector_coarse(key, part):
    key = jax.random.fold_in(key, 16)
    return dominant(key, COARSE // B, 0.3, 0.1).reshape(COARSE, B)


def plant(drawn, key, smallest, largest):
    shape = drawn.shape
    place = [jax.random.randint(jax.random.fold_in(key, axis), (), 0, shape[axis]) for axis in range(len(shape))]
    drawn = drawn.at[tuple(place)].set(smallest)
    longest = shape.index(max(shape))
    place[longest] = (place[longest] + 1) % shape[longest]
    return drawn.at[tuple(place)].set(largest)


def shard_levels(rng, extent, shards, smallest, high):
    def one(axis_at, blocks):
        heights = jax.random.uniform(jax.random.fold_in(jax.random.fold_in(rng, 6), axis_at), (blocks,), jnp.float32, smallest / len(shards), high / len(shards))
        return jnp.repeat(jnp.exp(heights), extent[axis_at] // blocks).reshape((-1,) + (1,) * (len(extent) - axis_at - 1))

    loudness = one(*shards[0])
    for cut in shards[1:]:
        loudness = loudness * one(*cut)
    return loudness


def centred(rng, extent, scale, bound, cuts=(), kind=jnp.bfloat16):
    level = shard_levels(rng, extent, cuts, -0.22, 0.18) if cuts else 1.0
    drawn = jax.random.normal(rng, extent, jnp.float32) * scale * level
    return jnp.minimum(jnp.maximum(drawn, -bound), bound).astype(kind)


def setup_inputs(seed: int = 0) -> dict:
    key_list = jax.random.split(jax.random.key(seed), 15)
    right_side = centred(key_list[0], (EDGES, R), 1.0, 6.0, ((0, 768),), jnp.float32)
    smoother = draw_smoother(jax.random.fold_in(key_list[14], 71), 0)
    diagonal_blocks = draw_diagonal_blocks(jax.random.fold_in(key_list[14], 71), 0)
    couplings = centred(key_list[3], (EDGE_BLOCKS, B, B), B ** -0.5, 0.5, ((0, 768),), jnp.float32)
    grad_blocks = centred(key_list[4], (EDGE_BLOCKS, 2, B, B), B ** -0.5, 0.5, ((0, 768),), jnp.float32)
    grad_pattern = plant(jax.random.randint(key_list[5], (EDGE_BLOCKS, 2), 0, NN + 1), jax.random.fold_in(key_list[5], 1), 0, NN).astype(jnp.int32)
    interp_blocks = centred(key_list[6], (EDGE_BLOCKS, 2, B, B), B ** -0.5, 0.5, ((0, 768),), jnp.float32)
    interp_pattern = plant(jax.random.randint(key_list[7], (EDGE_BLOCKS, 2), 0, NV + 1), jax.random.fold_in(key_list[7], 1), 0, NV).astype(jnp.int32)
    node_smoother = draw_node_smoother(jax.random.fold_in(key_list[14], 71), 0)
    vector_smoother = draw_vector_smoother(jax.random.fold_in(key_list[14], 71), 0)
    node_aggregates = plant(jax.random.randint(key_list[10], (NODES,), 0, B // 8), jax.random.fold_in(key_list[10], 1), 0, (B // 8) - 1).astype(jnp.int32)
    vector_aggregates = plant(jax.random.randint(key_list[11], (VEC_DOFS,), 0, 3 * B // 8), jax.random.fold_in(key_list[11], 1), 0, (3 * B // 8) - 1).astype(jnp.int32)
    node_coarse = draw_node_coarse(jax.random.fold_in(key_list[14], 71), 0)
    vector_coarse = draw_vector_coarse(jax.random.fold_in(key_list[14], 71), 0)
    return dict(right_side=right_side, smoother=smoother, diagonal_blocks=diagonal_blocks, couplings=couplings, grad_blocks=grad_blocks, grad_pattern=grad_pattern, interp_blocks=interp_blocks, interp_pattern=interp_pattern, node_smoother=node_smoother, vector_smoother=vector_smoother, node_aggregates=node_aggregates, vector_aggregates=vector_aggregates, node_coarse=node_coarse, vector_coarse=vector_coarse)


def multiply(formula, left, right):
    return jnp.einsum(formula, left, right, precision=lax.Precision.HIGHEST, preferred_element_type=jnp.float32)


def restrict_blocks(blocks, pattern, resid, amount):
    onehot = (pattern[:, :, None] == jnp.arange(amount + 1, dtype=jnp.int32)[None, None, :]).astype(jnp.float32)
    products_all = multiply('ksij,kir->ksjr', blocks, resid)
    return multiply('ksc,ksjr->cjr', onehot, products_all)


def prolong_blocks(blocks, pattern, extended, amount):
    onehot = (pattern[:, :, None] == jnp.arange(amount + 1, dtype=jnp.int32)[None, None, :]).astype(jnp.float32)
    picked = multiply('ksc,cjr->ksjr', onehot, extended)
    return multiply('ksij,ksjr->kir', blocks, picked)


def auxiliary_solve(aux_resid, block_smoother, aggregates, coarse_op):
    amount, width, vectors = aux_resid.shape
    fixed = multiply('cij,cjr->cir', block_smoother, aux_resid)
    onehot = (aggregates[:, None] == jnp.arange(width, dtype=jnp.int32)[None, :]).astype(jnp.float32)
    flattened = aux_resid.reshape(amount * width, vectors)
    coarse = multiply('nc,nr->cr', onehot, flattened)
    coarse_fix = multiply('ij,jr->ir', coarse_op, coarse)
    return fixed + multiply('nc,cr->nr', onehot, coarse_fix).reshape(amount, width, vectors)


def reference(right_side, smoother, diagonal_blocks, couplings, grad_blocks, grad_pattern, interp_blocks, interp_pattern, node_smoother, vector_smoother, node_aggregates, vector_aggregates, node_coarse, vector_coarse):
    regions = N_REGION
    source = right_side.reshape(EDGE_BLOCKS, B, R)
    smoothed = multiply('kij,kjr->kir', smoother, source)
    nothing = jnp.zeros((1, B, R), jnp.float32)
    following = jnp.concatenate([smoothed[1:], nothing], axis=0)
    forward = multiply('kij,kjr->kir', couplings, following)
    backward = jnp.concatenate([nothing, multiply('kji,kjr->kir', couplings[:-1], smoothed[:-1])], axis=0)
    resid = source - (multiply('kij,kjr->kir', diagonal_blocks, smoothed) + forward + backward)

    resid_reg = resid.reshape(regions, NB, B, R)
    grad_reg = grad_blocks.reshape(regions, NB, 2, B, B)
    interp_reg = interp_blocks.reshape(regions, NB, 2, B, B)
    gpat_reg = grad_pattern.reshape(regions, NB, 2)
    ppat_reg = interp_pattern.reshape(regions, NB, 2)

    def restrict_both(pieces):
        return (restrict_blocks(pieces[1], pieces[2], pieces[0], NN), restrict_blocks(pieces[3], pieces[4], pieces[0], NV))

    node_ext, vector_ext = lax.map(restrict_both, (resid_reg, grad_reg, gpat_reg, interp_reg, ppat_reg))
    node_in = jnp.concatenate([nothing, node_ext[:-1, NN]], axis=0)
    vector_in = jnp.concatenate([nothing, vector_ext[:-1, NV]], axis=0)
    node_resid = node_ext[:, :NN].at[:, 0].add(node_in)
    vector_resid = vector_ext[:, :NV].at[:, 0].add(vector_in)

    def solve_both(pieces):
        return (auxiliary_solve(pieces[0], pieces[1], pieces[2], pieces[3]), auxiliary_solve(pieces[4], pieces[5], pieces[6], pieces[7]))

    node_fix, vector_fix = lax.map(solve_both, (
        node_resid, node_smoother.reshape(regions, NN, B, B), node_aggregates.reshape(regions, NN * B), node_coarse.reshape(regions, B, B),
        vector_resid, vector_smoother.reshape(regions, NV, B, B), vector_aggregates.reshape(regions, NV * B), vector_coarse.reshape(regions, B, B)))

    node_next = jnp.concatenate([node_fix[1:, 0], nothing], axis=0)
    vector_next = jnp.concatenate([vector_fix[1:, 0], nothing], axis=0)
    node_extended = jnp.concatenate([node_fix, node_next[:, None]], axis=1)
    vector_extended = jnp.concatenate([vector_fix, vector_next[:, None]], axis=1)

    def prolong_both(pieces):
        return prolong_blocks(pieces[0], pieces[1], pieces[2], NN) + prolong_blocks(pieces[3], pieces[4], pieces[5], NV)

    added = lax.map(prolong_both, (grad_reg, gpat_reg, node_extended, interp_reg, ppat_reg, vector_extended))
    return (smoothed + added.reshape(EDGE_BLOCKS, B, R)).reshape(EDGES, R)
```

```python
import jax
import jax.numpy as jnp
from jax import lax
from jax.experimental import pallas as pl
from jax.experimental.pallas import tpu as pltpu
from jax.sharding import PartitionSpec as P

F32 = jnp.float32
BF16 = jnp.bfloat16
B = 128
SLOTS = 6
V_NEXT, NODE, N_NEXT = 3, 4, 5


def crossed(x, pairs):
    return lax.ppermute(x, "region", pairs)


def chip_pairs():
    size = lax.axis_size("region")
    swap = [(i, i ^ 1) for i in range(size)]
    ahead = [(i, i + 1) for i in range(1, size - 1, 2)]
    return swap, ahead, [(b, a) for a, b in ahead]


def is_second():
    return lax.axis_index("region") % 2 == 1


def by_core(first, second):
    pl.when(jnp.logical_not(is_second()))(first)
    pl.when(is_second())(second)


def split(x):
    high = x.astype(BF16)
    return high, (x - high.astype(F32)).astype(BF16)


def left(x):
    high, low = split(x)
    return jnp.concatenate([high, high, low], axis=1)


def right(x):
    high, low = split(x)
    return jnp.concatenate([high, low, high], axis=0)


def mul(x, y):
    return jnp.dot(x, y, preferred_element_type=F32)


def dot3(x, y):
    return mul(left(x), right(y))


def pack(x):
    return jnp.concatenate([x[:64], x[64:]], axis=1)


def unpack(x):
    return jnp.concatenate([x[:, :B], x[:, B:]], axis=0)


def transposed(blocks):
    return left(jnp.concatenate([x.T for x in blocks], axis=0))


def slots_of(gpat, ipat, k):
    return [NODE + gpat[0, k], NODE + gpat[1, k], ipat[0, k], ipat[1, k]]


def send_kernel(gfrom, ifrom, source, smoother, couplings, grad, interp, ahead, swap, gpat, ipat, last, first, mats, pairs, total, sems):
    moves = [
        (source.at[pl.ds(3 * B, B)], last),
        (smoother.at[3], mats.at[0]),
        (couplings.at[3], mats.at[1]),
        (grad.at[3], pairs.at[0]),
        (interp.at[3], pairs.at[1]),
        (gfrom, gpat),
        (ifrom, ipat),
        (source.at[pl.ds(0, B)], first),
        (smoother.at[0], mats.at[2]),
    ]
    copies = [pltpu.make_async_copy(a, b, sems.at[i]) for i, (a, b) in enumerate(moves)]
    for copy in copies:
        copy.start()
    for copy in copies[:3]:
        copy.wait()
    smoothed = dot3(mats[0], last[...])
    ahead[:B] = dot3(mats[1].T, smoothed)
    for copy in copies[3:]:
        copy.wait()

    def first_core():
        swap[...] = ahead[:B]

    def second_core():
        total[...] = jnp.zeros_like(total)
        for s in range(2):
            total[:, :B] += jnp.where(gpat[s, 3] == 1, pairs[0, s], 0.0)
            total[:, B:] += jnp.where(ipat[s, 3] == 3, pairs[1, s], 0.0)
        folded = dot3(total[...].T, mats[1])
        ahead[B:, : 2 * B] = pack(folded[:B])
        ahead[B:, 2 * B :] = pack(folded[B:])
        swap[...] = dot3(mats[2], first[...])

    by_core(first_core, second_core)


def resid_kernel(gpat, ipat, source, smoother, diagonal, couplings, grad, interp, smoothed, held, first_t, last_t):
    held[...] = jnp.zeros_like(held)
    resid = [source[k * B : (k + 1) * B] for k in range(4)]
    for k in range(4):
        got = dot3(smoother[k], source[k * B : (k + 1) * B])
        smoothed[k * B : (k + 1) * B] = got
        rows = [diagonal[k]]
        at = [k]
        if k:
            rows.append(couplings[k - 1])
            at.append(k - 1)
        if k < 3:
            rows.append(couplings[k].T)
            at.append(k + 1)
        terms = mul(left(jnp.concatenate(rows, axis=0)), right(got))
        for i, j in enumerate(at):
            resid[j] = resid[j] - terms[i * B : (i + 1) * B]
    for k in range(4):
        blocks = transposed([grad[k, 0], grad[k, 1], interp[k, 0], interp[k, 1]])
        if k == 0:
            first_t[...] = blocks
        if k == 3:
            last_t[...] = blocks
        terms = mul(blocks, right(resid[k]))
        for i, slot in enumerate(slots_of(gpat, ipat, k)):
            held[slot] += terms[i * B : (i + 1) * B]


def subtract(gpat, ipat, k, blocks, x, target):
    terms = mul(blocks, right(x))
    for i, slot in enumerate(slots_of(gpat, ipat, k)):
        target[slot] -= terms[i * B : (i + 1) * B]


def partial_kernel(gpat, ipat, came, couplings, first_t, last_t, held, out, partial):
    out[...] = held[...]

    def first_core():
        subtract(gpat, ipat, 3, last_t[...], dot3(couplings[3], came[...]), out)

    def second_core():
        subtract(gpat, ipat, 0, first_t[...], came[...], out)
        partial[:B] = out[V_NEXT]
        partial[B:] = out[N_NEXT]

    by_core(first_core, second_core)


def operator_kernel(gpat, ipat, nsm, vsm, nagg, vagg, ncoarse, vcoarse, grad, interp, smoothed, partial, node_op, vec_op, corner, wide, column, behind):
    behind[...] = smoothed[:B]

    def folded(aggregates, coarse):
        width = aggregates.shape[0]
        onehot = (lax.broadcasted_iota(jnp.int32, (B, width), 0) == aggregates[...][None, :]).astype(F32)
        high, low = split(coarse[...])
        pick = onehot.astype(BF16)
        cols = mul(jnp.concatenate([high, low], axis=1), jnp.concatenate([pick, pick], axis=0))
        back = onehot.T.astype(BF16)
        high, low = split(cols)
        return mul(jnp.concatenate([back, back], axis=1), jnp.concatenate([high, low], axis=0))

    n_op = nsm[0] + folded(nagg, ncoarse)
    node_op[...] = left(n_op)
    v_op = folded(vagg, vcoarse)
    zero = jnp.zeros((B, B), F32)
    v_op = v_op + jnp.concatenate(
        [jnp.concatenate([vsm[i] if i == j else zero for j in range(3)], axis=1) for i in range(3)], axis=0
    )
    vec_op[...] = left(v_op)
    corner[:, : 2 * B] = pack(v_op[:B, :B])
    corner[:, 2 * B :] = pack(n_op)
    wide[...] = jnp.zeros_like(wide)
    for k in range(4):
        slots = slots_of(gpat, ipat, k)
        blocks = [grad[k, 0], grad[k, 1], interp[k, 0], interp[k, 1]]
        for slot, block in zip(slots, blocks):
            wide[slot, k * B : (k + 1) * B] += block
    vec = jnp.concatenate([wide[0], wide[1], wide[2]], axis=1)
    column[:, :B] = dot3(vec, v_op[:, :B])
    column[:, B:] = dot3(wide[NODE], n_op)


def fix_all(work, node_op, vec_op, corner, fix, back, full):
    vec = mul(vec_op[...], right(jnp.concatenate([work[0], work[1], work[2]], axis=0)))
    node = mul(node_op[...], right(work[NODE]))
    fix[: 3 * B] = vec
    fix[3 * B :] = node
    back[:B] = vec[:B]
    back[B : 2 * B] = node
    back[2 * B :] = corner[...]
    full[:B] = work[V_NEXT]
    full[B:] = work[N_NEXT]


def first_fix_kernel(gpat, ipat, came, first_t, held, node_op, vec_op, corner, fix, back, full, work):
    def first_core():
        work[...] = held[...]
        subtract(gpat, ipat, 0, first_t[...], came[:B], work)
        fix_all(work, node_op, vec_op, corner, fix, back, full)

    pl.when(jnp.logical_not(is_second()))(first_core)


def second_fix_kernel(gpat, ipat, came, couplings, last_t, held, node_op, vec_op, corner, full_first, fix, full, swap, work):
    def first_core():
        swap[: 2 * B] = full_first[...]

    def second_core():
        work[...] = held[...]
        subtract(gpat, ipat, 3, last_t[...], dot3(couplings[3], came[...]), work)
        fix_all(work, node_op, vec_op, corner, fix, swap, full)

    by_core(first_core, second_core)


def base_kernel(smoothed, fix_first, fix_second, wide, ahead, came, column, out):
    here = [wide[0], wide[1], wide[2], wide[NODE]]

    def first_core():
        mats = ahead[B:]
        folded = jnp.concatenate([unpack(mats[:, 2 * B :]), unpack(mats[:, : 2 * B])], axis=0)
        partial = came[...] - dot3(folded, smoothed[:B])
        blocks = jnp.concatenate([*here, column[...]], axis=1)
        out[...] = smoothed[...] + dot3(blocks, jnp.concatenate([fix_first[...], partial], axis=0))

    def second_core():
        out[...] = smoothed[...] + dot3(jnp.concatenate(here, axis=1), fix_second[...])

    by_core(first_core, second_core)


def next_fix(came, full):
    corner = came[2 * B :]
    vec = came[:B] + dot3(unpack(corner[:, : 2 * B]), full[:B])
    node = came[B : 2 * B] + dot3(unpack(corner[:, 2 * B :]), full[B:])
    return [vec, node]


def last_kernel(came_swap, came_back, full_first, full_second, wide, column, base, out):
    ahead = [wide[V_NEXT], wide[N_NEXT]]

    def first_core():
        rows = next_fix(came_swap, full_first)
        out[...] = base[...] + dot3(jnp.concatenate(ahead, axis=1), jnp.concatenate(rows, axis=0))

    def second_core():
        rows = next_fix(came_back, full_second)
        blocks = jnp.concatenate([*ahead, column[...]], axis=1)
        out[...] = base[...] + dot3(blocks, jnp.concatenate([*rows, came_swap[: 2 * B]], axis=0))

    by_core(first_core, second_core)


VMEM = pl.BlockSpec(memory_space=pltpu.VMEM)
SMEM = pl.BlockSpec(memory_space=pltpu.SMEM)
HBM = pl.BlockSpec(memory_space=pltpu.HBM)
ANY = pl.BlockSpec(memory_space=pl.ANY)


def call(kernel, outs, in_specs, *args, scratch=(), units=0):
    return pl.pallas_call(
        kernel,
        out_shape=[jax.ShapeDtypeStruct(shape, dtype) for shape, dtype in outs],
        in_specs=in_specs,
        out_specs=[VMEM] * len(outs),
        scratch_shapes=list(scratch),
        compiler_params=pltpu.CompilerParams(vmem_limit_bytes=24 * 1024 * 1024),
        cost_estimate=pl.CostEstimate(flops=units * 50331648, bytes_accessed=units, transcendentals=0),
    )(*args)


def local(
    right_side,
    smoother,
    diagonal_blocks,
    couplings,
    grad_blocks,
    grad_pattern,
    interp_blocks,
    interp_pattern,
    node_smoother,
    vector_smoother,
    node_aggregates,
    vector_aggregates,
    node_coarse,
    vector_coarse,
):
    vectors = right_side.shape[1]
    pats = (grad_pattern.T, interp_pattern.T)

    swap, ahead, behind = chip_pairs()

    sent_ahead, sent_swap = call(
        send_kernel,
        [((B + 64, vectors), F32), ((B, vectors), F32)],
        [HBM] * 7,
        *(
            pltpu.with_memory_space_constraint(x, pltpu.HBM)
            for x in (*pats, right_side, smoother, couplings, grad_blocks, interp_blocks)
        ),
        scratch=[
            pltpu.SMEM((2, 4), jnp.int32),
            pltpu.SMEM((2, 4), jnp.int32),
            pltpu.VMEM((B, vectors), F32),
            pltpu.VMEM((B, vectors), F32),
            pltpu.VMEM((3, B, B), F32),
            pltpu.VMEM((2, 2, B, B), F32),
            pltpu.VMEM((B, 2 * B), F32),
            pltpu.SemaphoreType.DMA((9,)),
        ],
    )
    came_ahead = crossed(sent_ahead, ahead)
    came_swap = crossed(sent_swap, swap)

    smoothed, held, first_t, last_t = call(
        resid_kernel,
        [((4 * B, vectors), F32), ((SLOTS, B, vectors), F32), ((4 * B, 3 * B), BF16), ((4 * B, 3 * B), BF16)],
        [SMEM] * 2 + [VMEM] * 6,
        *pats, right_side, smoother, diagonal_blocks, couplings, grad_blocks, interp_blocks,
        units=30,
    )
    held, partial = call(
        partial_kernel,
        [((SLOTS, B, vectors), F32), ((2 * B, vectors), F32)],
        [SMEM] * 2 + [VMEM] * 5,
        *pats, came_swap, couplings, first_t, last_t, held,
        units=0,
    )
    came_partial = crossed(partial, ahead)

    node_op, vec_op, corner, wide, column, sent_behind = call(
        operator_kernel,
        [
            ((B, 3 * B), BF16),
            ((3 * B, 9 * B), BF16),
            ((64, vectors), F32),
            ((SLOTS, 4 * B, B), F32),
            ((4 * B, 2 * B), F32),
            ((B, vectors), F32),
        ],
        [SMEM] * 2 + [VMEM] * 9 + [ANY],
        *pats, node_smoother, vector_smoother, node_aggregates, vector_aggregates,
        node_coarse, vector_coarse, grad_blocks, interp_blocks, smoothed, partial,
        units=0,
    )
    came_behind = crossed(sent_behind, behind)
    sizes = [((4 * B, vectors), F32), ((2 * B + 64, vectors), F32), ((2 * B, vectors), F32)]
    work = [pltpu.VMEM((SLOTS, B, vectors), F32)]
    fix_first, sent_back, full_first = call(
        first_fix_kernel,
        sizes,
        [SMEM] * 2 + [VMEM] * 6,
        *pats, came_ahead, first_t, held, node_op, vec_op, corner,
        scratch=work,
        units=100,
    )
    came_back = crossed(sent_back, behind)
    fix_second, full_second, sent_swap = call(
        second_fix_kernel,
        [sizes[0], sizes[2], sizes[1]],
        [SMEM] * 2 + [VMEM] * 8,
        *pats, came_behind, couplings, last_t, held, node_op, vec_op, corner, full_first,
        scratch=work,
        units=0,
    )
    came_swap = crossed(sent_swap, swap)
    (base,) = call(
        base_kernel,
        [((4 * B, vectors), F32)],
        [VMEM] * 7,
        smoothed, fix_first, fix_second, wide, came_ahead, came_partial, column,
        units=60,
    )
    (out,) = call(
        last_kernel,
        [((4 * B, vectors), F32)],
        [VMEM] * 7,
        came_swap, came_back, full_first, full_second, wide, column, base,
    )
    return out


def solution(mesh):
    in_specs = (
        P("region", None),
        P("region", None, None),
        P("region", None, None),
        P("region", None, None),
        P("region", None, None, None),
        P("region", None),
        P("region", None, None, None),
        P("region", None),
        P("region", None, None),
        P("region", None, None),
        P("region"),
        P("region"),
        P("region", None),
        P("region", None),
    )
    out_specs = P("region", None)
    return jax.shard_map(local, mesh=mesh, in_specs=in_specs, out_specs=out_specs, check_vma=False)
```

```python
import jax
import jax.numpy as jnp
from jax import lax
from jax.experimental import pallas as pl
from jax.experimental.pallas import tpu as pltpu
from jax.sharding import PartitionSpec as P

F32 = jnp.float32
BF16 = jnp.bfloat16
B = 128
SLOTS = 6
V_NEXT, NODE, N_NEXT = 3, 4, 5


def crossed(x, pairs):
    return lax.ppermute(x, "region", pairs)


def chip_pairs():
    size = lax.axis_size("region")
    swap = [(i, i ^ 1) for i in range(size)]
    ahead = [(i, i + 1) for i in range(1, size - 1, 2)]
    return swap, ahead, [(b, a) for a, b in ahead]


def is_second():
    return lax.axis_index("region") % 2 == 1


def by_core(first, second):
    pl.when(jnp.logical_not(is_second()))(first)
    pl.when(is_second())(second)


def split(x):
    high = x.astype(BF16)
    return high, (x - high.astype(F32)).astype(BF16)


def left(x):
    high, low = split(x)
    return jnp.concatenate([high, high, low], axis=1)


def right(x):
    high, low = split(x)
    return jnp.concatenate([high, low, high], axis=0)


def mul(x, y):
    return jnp.dot(x, y, preferred_element_type=F32)


def dot3(x, y):
    return mul(left(x), right(y))


def pack(x):
    return jnp.concatenate([x[:64], x[64:]], axis=1)


def unpack(x):
    return jnp.concatenate([x[:, :B], x[:, B:]], axis=0)


def transposed(blocks):
    return left(jnp.concatenate([x.T for x in blocks], axis=0))


def slots_of(gpat, ipat, k):
    return [NODE + gpat[0, k], NODE + gpat[1, k], ipat[0, k], ipat[1, k]]


def fetched(gfrom, ifrom, gpat, ipat, sems):
    copies = [pltpu.make_async_copy(gfrom, gpat, sems.at[0]), pltpu.make_async_copy(ifrom, ipat, sems.at[1])]
    for copy in copies:
        copy.start()
    return copies


def wait_all(copies):
    for copy in copies:
        copy.wait()


def named(pattern, s, k, block, value):
    return jnp.where(pattern[s : s + 1, k : k + 1] == value, block, 0.0)


def send_kernel(
    gfrom, ifrom, source, smoother, couplings, grad, interp, diagonal_from, ahead, swap, diagonal,
    gpat, ipat, last, first, mats, pairs, total, sems
):
    moves = [
        (source.at[pl.ds(3 * B, B)], last),
        (smoother.at[3], mats.at[0]),
        (couplings.at[3], mats.at[1]),
        (grad.at[3], pairs.at[0]),
        (interp.at[3], pairs.at[1]),
        (gfrom, gpat),
        (ifrom, ipat),
        (source.at[pl.ds(0, B)], first),
        (smoother.at[0], mats.at[2]),
        (diagonal_from, diagonal),
    ]
    copies = [pltpu.make_async_copy(a, b, sems.at[i]) for i, (a, b) in enumerate(moves)]
    for copy in copies:
        copy.start()
    wait_all(copies[:-1])
    smoothed = dot3(mats[0], last[...])
    beside = dot3(mats[2], first[...])
    total[...] = jnp.zeros_like(total)
    for s in range(2):
        total[:, :B] += named(gpat, s, 3, pairs[0, s], 1)
        total[:, B:] += named(ipat, s, 3, pairs[1, s], 3)
    folded = dot3(total[...].T, mats[1])
    ahead[B:, : 2 * B] = pack(folded[:B])
    ahead[B:, 2 * B :] = pack(folded[B:])
    onward = dot3(mats[1].T, smoothed)
    ahead[:B] = onward
    swap[...] = jnp.where(is_second(), beside, onward)
    copies[-1].wait()


def resid_kernel(gpat, ipat, source, smoother, diagonal, couplings, grad, interp, smoothed, resid, named_next, total):
    for k in range(4):
        smoothed[k * B : (k + 1) * B] = dot3(smoother[k], source[k * B : (k + 1) * B])
        rows = slice(k * B, (k + 1) * B)
        total[rows, :B] = sum(named(ipat, s, k, interp[k, s], 3) for s in range(2))
        total[rows, B:] = sum(named(gpat, s, k, grad[k, s], 1) for s in range(2))
    named_next[...] = left(total[...].T)
    zero = jnp.zeros((B, B), F32)
    rows = []
    for k in range(4):
        row = [zero] * 4
        row[k] = diagonal[k]
        if k:
            row[k - 1] = couplings[k - 1].T
        if k < 3:
            row[k + 1] = couplings[k]
        rows.append(jnp.concatenate(row, axis=1))
    resid[...] = source[...] - mul(left(jnp.concatenate(rows, axis=0)), right(smoothed[...]))


def partial_kernel(came, resid, named_next, partial):
    def second_core():
        whole = jnp.concatenate([resid[:B] - came[...], resid[B:]], axis=0)
        partial[...] = mul(named_next[...], right(whole))

    pl.when(is_second())(second_core)


def subtract(gpat, ipat, k, blocks, x, target, pats=()):
    terms = mul(blocks, right(x))
    wait_all(pats)
    for i, slot in enumerate(slots_of(gpat, ipat, k)):
        target[slot] -= terms[i * B : (i + 1) * B]


def operators(gpat, ipat, nsm, vsm, nagg, vagg, ncoarse, vcoarse, grad, interp, node_op, vec_op, corner, wide, column):
    def folded(aggregates, coarse):
        width = aggregates.shape[0]
        onehot = (lax.broadcasted_iota(jnp.int32, (B, width), 0) == aggregates[...][None, :]).astype(F32)
        high, low = split(coarse[...])
        pick = onehot.astype(BF16)
        cols = mul(jnp.concatenate([high, low], axis=1), jnp.concatenate([pick, pick], axis=0))
        back = onehot.T.astype(BF16)
        high, low = split(cols)
        return mul(jnp.concatenate([back, back], axis=1), jnp.concatenate([high, low], axis=0))

    n_op = nsm[0] + folded(nagg, ncoarse)
    node_op[...] = left(n_op)
    v_op = folded(vagg, vcoarse)
    zero = jnp.zeros((B, B), F32)
    v_op = v_op + jnp.concatenate(
        [jnp.concatenate([vsm[i] if i == j else zero for j in range(3)], axis=1) for i in range(3)], axis=0
    )
    vec_op[...] = left(v_op)
    corner[:, : 2 * B] = pack(v_op[:B, :B])
    corner[:, 2 * B :] = pack(n_op)
    wide[...] = jnp.zeros_like(wide)
    for k in range(4):
        slots = slots_of(gpat, ipat, k)
        blocks = [grad[k, 0], grad[k, 1], interp[k, 0], interp[k, 1]]
        for slot, block in zip(slots, blocks):
            wide[slot, k * B : (k + 1) * B] += block
    vec = jnp.concatenate([wide[0], wide[1], wide[2]], axis=1)
    column[:, :B] = dot3(vec, v_op[:, :B])
    column[:, B:] = dot3(wide[NODE], n_op)


def fix_all(work, node_op, vec_op, corner, fix, back, full):
    vec = mul(vec_op[...], right(jnp.concatenate([work[0], work[1], work[2]], axis=0)))
    node = mul(node_op[...], right(work[NODE]))
    fix[: 3 * B] = vec
    fix[3 * B :] = node
    back[:B] = vec[:B]
    back[B : 2 * B] = node
    back[2 * B : 2 * B + 64] = corner[...]
    full[:B] = work[V_NEXT]
    full[B:] = work[N_NEXT]


def prepare(keep, gfrom, ifrom, *refs):
    mats, (resid, came, couplings), outs = refs[:8], refs[8:11], refs[12:]
    node_op, vec_op, corner, wide, column, held, kept, gpat, ipat, sems = outs
    grad, interp = mats[6:]
    wait_all(fetched(gfrom, ifrom, gpat, ipat, sems))
    operators(gpat, ipat, *mats, node_op, vec_op, corner, wide, column)
    held[...] = jnp.zeros_like(held)
    for k in range(4):
        blocks = transposed([grad[k, 0], grad[k, 1], interp[k, 0], interp[k, 1]])
        if k == keep:
            kept[...] = blocks
        rows = resid[k * B : (k + 1) * B]
        if keep == 0 and k == 3:
            rows = rows - dot3(couplings[3], came[...])
        if keep == 3 and k == 0:
            rows = rows - came[...]
        terms = mul(blocks, right(rows))
        for i, slot in enumerate(slots_of(gpat, ipat, k)):
            held[slot] += terms[i * B : (i + 1) * B]


def first_prepare_kernel(*refs):
    pl.when(jnp.logical_not(is_second()))(lambda: prepare(0, *refs))


def second_prepare_kernel(*refs):
    pl.when(is_second())(lambda: prepare(3, *refs))


def first_fix_kernel(
    gfrom, ifrom, came, first_t, held, node_op, vec_op, corner, smoothed, fix, back, full, behind, gpat, ipat, sems, work
):
    def first_core():
        pats = fetched(gfrom, ifrom, gpat, ipat, sems)
        behind[...] = smoothed[:B]
        work[...] = held[...]
        subtract(gpat, ipat, 0, first_t[...], came[:B], work, pats)
        fix_all(work, node_op, vec_op, corner, fix, back, full)

    pl.when(jnp.logical_not(is_second()))(first_core)


def second_fix_kernel(
    gfrom, ifrom, came, couplings, last_t, held, node_op, vec_op, corner, full_first, fix, full, swap, gpat, ipat, sems, work
):
    def first_core():
        swap[: 2 * B] = full_first[...]

    def second_core():
        pats = fetched(gfrom, ifrom, gpat, ipat, sems)
        work[...] = held[...]
        subtract(gpat, ipat, 3, last_t[...], dot3(couplings[3], came[...]), work, pats)
        fix_all(work, node_op, vec_op, corner, fix, swap, full)

    by_core(first_core, second_core)


def base_kernel(smoothed, fix_first, fix_second, wide_first, wide_second, ahead, came, column, out):
    def first_core():
        mats = ahead[B:]
        folded = jnp.concatenate([unpack(mats[:, 2 * B :]), unpack(mats[:, : 2 * B])], axis=0)
        partial = came[...] - dot3(folded, smoothed[:B])
        blocks = jnp.concatenate([*here(wide_first), column[...]], axis=1)
        out[...] = smoothed[...] + dot3(blocks, jnp.concatenate([fix_first[...], partial], axis=0))

    def second_core():
        out[...] = smoothed[...] + dot3(jnp.concatenate(here(wide_second), axis=1), fix_second[...])

    by_core(first_core, second_core)


def here(wide):
    return [wide[0], wide[1], wide[2], wide[NODE]]


def next_fix(came, full):
    corner = came[2 * B : 2 * B + 64]
    vec = came[:B] + dot3(unpack(corner[:, : 2 * B]), full[:B])
    node = came[B : 2 * B] + dot3(unpack(corner[:, 2 * B :]), full[B:])
    return [vec, node]


def next_term(came, full, wide):
    blocks = jnp.concatenate([wide[V_NEXT], wide[N_NEXT]], axis=1)
    return dot3(blocks, jnp.concatenate(next_fix(came, full), axis=0))


def first_end_kernel(came, full, wide, column, base, out, more, work, sem):
    def first_core():
        work[...] = base[...] + next_term(came, full, wide)
        copy = pltpu.make_async_copy(work, out, sem)
        copy.start()
        copy.wait()

    def second_core():
        more[...] = base[...] + dot3(column[...], came[: 2 * B])

    by_core(first_core, second_core)


def second_end_kernel(came, full, wide, more, _, out, work, sem):
    def second_core():
        work[...] = more[...] + next_term(came, full, wide)
        copy = pltpu.make_async_copy(work, out, sem)
        copy.start()
        copy.wait()

    pl.when(is_second())(second_core)


VMEM = pl.BlockSpec(memory_space=pltpu.VMEM)
HBM = pl.BlockSpec(memory_space=pltpu.HBM)
ANY = pl.BlockSpec(memory_space=pl.ANY)

PATTERNS = [pltpu.SMEM((2, 4), jnp.int32), pltpu.SMEM((2, 4), jnp.int32), pltpu.SemaphoreType.DMA((2,))]


def call(kernel, outs, in_specs, *args, scratch=(), units=0, out_specs=None, aliases=None):
    return pl.pallas_call(
        kernel,
        out_shape=[jax.ShapeDtypeStruct(shape, dtype) for shape, dtype in outs],
        in_specs=in_specs,
        out_specs=out_specs or [VMEM] * len(outs),
        input_output_aliases=aliases or {},
        scratch_shapes=list(scratch),
        compiler_params=pltpu.CompilerParams(vmem_limit_bytes=24 * 1024 * 1024),
        cost_estimate=pl.CostEstimate(flops=units * 50331648, bytes_accessed=units, transcendentals=0),
    )(*args)


def local(
    right_side,
    smoother,
    diagonal_blocks,
    couplings,
    grad_blocks,
    grad_pattern,
    interp_blocks,
    interp_pattern,
    node_smoother,
    vector_smoother,
    node_aggregates,
    vector_aggregates,
    node_coarse,
    vector_coarse,
):
    vectors = right_side.shape[1]
    pats = (grad_pattern.T, interp_pattern.T)

    swap, ahead, behind = chip_pairs()

    sent_ahead, sent_swap, diagonal = call(
        send_kernel,
        [((B + 64, vectors), F32), ((B, vectors), F32), ((4, B, B), F32)],
        [HBM] * 8,
        *(
            pltpu.with_memory_space_constraint(x, pltpu.HBM)
            for x in (*pats, right_side, smoother, couplings, grad_blocks, interp_blocks, diagonal_blocks)
        ),
        scratch=[
            pltpu.VMEM((2, 4), jnp.int32),
            pltpu.VMEM((2, 4), jnp.int32),
            pltpu.VMEM((B, vectors), F32),
            pltpu.VMEM((B, vectors), F32),
            pltpu.VMEM((3, B, B), F32),
            pltpu.VMEM((2, 2, B, B), F32),
            pltpu.VMEM((B, 2 * B), F32),
            pltpu.SemaphoreType.DMA((10,)),
        ],
    )
    came_ahead = crossed(sent_ahead, ahead)
    came_swap = crossed(sent_swap, swap)

    smoothed, resid, named_next = call(
        resid_kernel,
        [((4 * B, vectors), F32), ((4 * B, vectors), F32), ((2 * B, 12 * B), BF16)],
        [VMEM] * 8,
        *pats, right_side, smoother, diagonal, couplings, grad_blocks, interp_blocks,
        scratch=[pltpu.VMEM((4 * B, 2 * B), F32)],
        units=30,
    )
    (partial,) = call(
        partial_kernel,
        [((2 * B, vectors), F32)],
        [VMEM] * 3,
        came_swap, resid, named_next,
        units=0,
    )
    came_partial = crossed(partial, ahead)

    mats = (node_smoother, vector_smoother, node_aggregates, vector_aggregates, node_coarse, vector_coarse, grad_blocks, interp_blocks)
    prepared = [
        ((B, 3 * B), BF16),
        ((3 * B, 9 * B), BF16),
        ((64, vectors), F32),
        ((SLOTS, 4 * B, B), F32),
        ((4 * B, 2 * B), F32),
        ((SLOTS, B, vectors), F32),
        ((4 * B, 3 * B), BF16),
    ]
    sizes = [((4 * B, vectors), F32), ((2 * B + 64, vectors), F32), ((2 * B, vectors), F32), ((B, vectors), F32)]
    longer = ((2 * B + 72, vectors), F32)
    work = pltpu.VMEM((SLOTS, B, vectors), F32)
    node_op, vec_op, corner, wide_first, column_first, held, first_t = call(
        first_prepare_kernel,
        prepared,
        [ANY] * 2 + [VMEM] * 11 + [ANY],
        *pats, *mats, resid, came_swap, couplings, partial,
        scratch=PATTERNS,
        units=0,
    )
    fix_first, sent_back, full_first, sent_behind = call(
        first_fix_kernel,
        [sizes[0], longer, *sizes[2:]],
        [ANY] * 2 + [VMEM] * 7,
        *pats, came_ahead, first_t, held, node_op, vec_op, corner, smoothed,
        scratch=[*PATTERNS, work],
        units=0,
    )
    came_behind = crossed(sent_behind, behind)
    came_back = crossed(sent_back, behind)
    node_op, vec_op, corner, wide_second, column_second, held, last_t = call(
        second_prepare_kernel,
        prepared,
        [ANY] * 2 + [VMEM] * 11 + [ANY],
        *pats, *mats, resid, came_swap, couplings, sent_back,
        scratch=PATTERNS,
        units=100,
    )
    fix_second, full_second, sent_swap = call(
        second_fix_kernel,
        [sizes[0], sizes[2], sizes[1]],
        [ANY] * 2 + [VMEM] * 8,
        *pats, came_behind, couplings, last_t, held, node_op, vec_op, corner, full_first,
        scratch=[*PATTERNS, work],
        units=0,
    )
    came_swap = crossed(sent_swap, swap)
    (base,) = call(
        base_kernel,
        [((4 * B, vectors), F32)],
        [VMEM] * 8,
        smoothed, fix_first, fix_second, wide_first, wide_second, came_ahead, came_partial, column_first,
        units=60,
    )
    work = [pltpu.VMEM((4 * B, vectors), F32), pltpu.SemaphoreType.DMA]
    out, more = call(
        first_end_kernel,
        [((4 * B, vectors), F32)] * 2,
        [VMEM] * 5,
        came_swap, full_first, wide_first, column_second, base,
        scratch=work,
        out_specs=[ANY, VMEM],
        units=0,
    )
    (out,) = call(
        second_end_kernel,
        [((4 * B, vectors), F32)],
        [VMEM] * 4 + [ANY],
        came_back, full_second, wide_second, more, out,
        scratch=work,
        out_specs=[ANY],
        aliases={4: 0},
    )
    return out


def solution(mesh):
    in_specs = (
        P("region", None),
        P("region", None, None),
        P("region", None, None),
        P("region", None, None),
        P("region", None, None, None),
        P("region", None),
        P("region", None, None, None),
        P("region", None),
        P("region", None, None),
        P("region", None, None),
        P("region"),
        P("region"),
        P("region", None),
        P("region", None),
    )
    out_specs = P("region", None)
    return jax.shard_map(local, mesh=mesh, in_specs=in_specs, out_specs=out_specs, check_vma=False)
```

```python
import jax
import jax.numpy as jnp
from jax import lax
from jax.experimental import pallas as pl
from jax.experimental.pallas import tpu as pltpu
from jax.sharding import PartitionSpec as P

F32 = jnp.float32
BF16 = jnp.bfloat16
B = 128
SLOTS = 6
V_NEXT, NODE, N_NEXT = 3, 4, 5


def crossed(x, pairs):
    return lax.ppermute(x, "region", pairs)


def chip_pairs():
    size = lax.axis_size("region")
    swap = [(i, i ^ 1) for i in range(size)]
    ahead = [(i, i + 1) for i in range(1, size - 1, 2)]
    return swap, ahead, [(b, a) for a, b in ahead]


def is_second():
    return lax.axis_index("region") % 2 == 1


def by_core(first, second):
    pl.when(jnp.logical_not(is_second()))(first)
    pl.when(is_second())(second)


def split(x):
    high = x.astype(BF16)
    return high, (x - high.astype(F32)).astype(BF16)


def left(x):
    high, low = split(x)
    return jnp.concatenate([high, high, low], axis=1)


def right(x):
    high, low = split(x)
    return jnp.concatenate([high, low, high], axis=0)


def mul(x, y):
    return jnp.dot(x, y, preferred_element_type=F32)


def dot3(x, y):
    return mul(left(x), right(y))


def pack(x):
    return jnp.concatenate([x[:64], x[64:]], axis=1)


def unpack(x):
    return jnp.concatenate([x[:, :B], x[:, B:]], axis=0)


def transposed(blocks):
    return left(jnp.concatenate([x.T for x in blocks], axis=0))


def slots_of(gpat, ipat, k):
    return [NODE + gpat[0, k], NODE + gpat[1, k], ipat[0, k], ipat[1, k]]


def fetched(gfrom, ifrom, gpat, ipat, sems):
    copies = [pltpu.make_async_copy(gfrom, gpat, sems.at[0]), pltpu.make_async_copy(ifrom, ipat, sems.at[1])]
    for copy in copies:
        copy.start()
    return copies


def wait_all(copies):
    for copy in copies:
        copy.wait()


def named(pattern, s, k, block, value):
    return jnp.where(pattern[s : s + 1, k : k + 1] == value, block, 0.0)


def send_kernel(
    source, smoother, couplings, diagonal_from, grad_from, interp_from, ahead, swap, diagonal, grad, interp, last, first, mats, sems
):
    moves = [
        (source.at[pl.ds(3 * B, B)], last),
        (smoother.at[3], mats.at[0]),
        (couplings.at[3], mats.at[1]),
        (source.at[pl.ds(0, B)], first),
        (smoother.at[0], mats.at[2]),
        (diagonal_from, diagonal),
        (grad_from, grad),
        (interp_from, interp),
    ]
    copies = [pltpu.make_async_copy(a, b, sems.at[i]) for i, (a, b) in enumerate(moves)]
    for copy in copies:
        copy.start()
    wait_all(copies[:5])
    smoothed = dot3(mats[0], last[...])
    beside = dot3(mats[2], first[...])
    onward = dot3(mats[1].T, smoothed)
    ahead[:B] = onward
    swap[...] = jnp.where(is_second(), beside, onward)
    wait_all(copies[5:])


def resid_kernel(gpat, ipat, source, smoother, diagonal, couplings, grad, interp, smoothed, resid, named_next, folded, total):
    for k in range(4):
        smoothed[k * B : (k + 1) * B] = dot3(smoother[k], source[k * B : (k + 1) * B])
        rows = slice(k * B, (k + 1) * B)
        total[rows, :B] = sum(named(ipat, s, k, interp[k, s], 3) for s in range(2))
        total[rows, B:] = sum(named(gpat, s, k, grad[k, s], 1) for s in range(2))
    next_t = total[...].T
    named_next[...] = left(next_t)
    mats = dot3(next_t[:, 3 * B :], couplings[3])
    folded[:, : 2 * B] = pack(mats[:B])
    folded[:, 2 * B :] = pack(mats[B:])
    zero = jnp.zeros((B, B), F32)
    high, low = split(smoothed[...])
    for half in range(2):
        rows = []
        for k in (2 * half, 2 * half + 1):
            row = [zero] * 3
            row[k - half] = diagonal[k]
            if k:
                row[k - half - 1] = couplings[k - 1].T if k - half else row[k - half - 1]
            if k - half < 2:
                row[k - half + 1] = couplings[k]
            rows.append(jnp.concatenate(row, axis=1))
        here = slice(half * B, (half + 3) * B)
        got = jnp.concatenate([high[here], low[here], high[here]], axis=0)
        at = slice(2 * half * B, 2 * (half + 1) * B)
        resid[at] = source[at] - mul(left(jnp.concatenate(rows, axis=0)), got)


def partial_kernel(came, resid, named_next, folded, partial):
    def second_core():
        whole = jnp.concatenate([resid[:B] - came[...], resid[B:]], axis=0)
        partial[: 2 * B] = mul(named_next[...], right(whole))
        partial[2 * B :] = folded[...]

    pl.when(is_second())(second_core)


def subtract(blocks, x, held, work):
    terms = mul(blocks, right(x))
    for slot in range(SLOTS):
        work[slot] = held[slot] - terms[slot * B : (slot + 1) * B]


def operators(gpat, ipat, nsm, vsm, nagg, vagg, ncoarse, vcoarse, grad, interp, node_op, vec_op, corner, wide, column):
    def folded(aggregates, coarse):
        width = aggregates.shape[0]
        onehot = (lax.broadcasted_iota(jnp.int32, (B, width), 0) == aggregates[...][None, :]).astype(F32)
        high, low = split(coarse[...])
        pick = onehot.astype(BF16)
        cols = mul(jnp.concatenate([high, low], axis=1), jnp.concatenate([pick, pick], axis=0))
        back = onehot.T.astype(BF16)
        high, low = split(cols)
        return mul(jnp.concatenate([back, back], axis=1), jnp.concatenate([high, low], axis=0))

    n_op = nsm[0] + folded(nagg, ncoarse)
    node_op[...] = left(n_op)
    v_op = folded(vagg, vcoarse)
    zero = jnp.zeros((B, B), F32)
    v_op = v_op + jnp.concatenate(
        [jnp.concatenate([vsm[i] if i == j else zero for j in range(3)], axis=1) for i in range(3)], axis=0
    )
    vec_op[...] = left(v_op)
    corner[:, : 2 * B] = pack(v_op[:B, :B])
    corner[:, 2 * B :] = pack(n_op)
    wide[...] = jnp.zeros_like(wide)
    for k in range(4):
        slots = slots_of(gpat, ipat, k)
        blocks = [grad[k, 0], grad[k, 1], interp[k, 0], interp[k, 1]]
        for slot, block in zip(slots, blocks):
            wide[slot, k * B : (k + 1) * B] += block
    vec = jnp.concatenate([wide[0], wide[1], wide[2]], axis=1)
    column[:, :B] = dot3(vec, v_op[:, :B])
    column[:, B:] = dot3(wide[NODE], n_op)


def fix_all(work, node_op, vec_op, corner, fix, back, full):
    vec = mul(vec_op[...], right(jnp.concatenate([work[0], work[1], work[2]], axis=0)))
    node = mul(node_op[...], right(work[NODE]))
    fix[: 3 * B] = vec
    fix[3 * B :] = node
    back[:B] = vec[:B]
    back[B : 2 * B] = node
    back[2 * B : 2 * B + 64] = corner[...]
    full[:B] = work[V_NEXT]
    full[B:] = work[N_NEXT]


def prepare(keep, gfrom, ifrom, *refs):
    mats, (resid, came, couplings), outs = refs[:8], refs[8:11], refs[12:]
    node_op, vec_op, corner, wide, column, held, kept, gpat, ipat, sems = outs
    grad, interp = mats[6:]
    wait_all(fetched(gfrom, ifrom, gpat, ipat, sems))
    operators(gpat, ipat, *mats, node_op, vec_op, corner, wide, column)
    kept[...] = transposed([wide[slot, keep * B : (keep + 1) * B] for slot in range(SLOTS)])
    held[...] = jnp.zeros_like(held)
    for k in range(4):
        blocks = transposed([grad[k, 0], grad[k, 1], interp[k, 0], interp[k, 1]])
        rows = resid[k * B : (k + 1) * B]
        if keep == 0 and k == 3:
            rows = rows - dot3(couplings[3], came[...])
        if keep == 3 and k == 0:
            rows = rows - came[...]
        terms = mul(blocks, right(rows))
        for i, slot in enumerate(slots_of(gpat, ipat, k)):
            held[slot] += terms[i * B : (i + 1) * B]


def first_prepare_kernel(*refs):
    pl.when(jnp.logical_not(is_second()))(lambda: prepare(0, *refs))


def second_prepare_kernel(*refs):
    pl.when(is_second())(lambda: prepare(3, *refs))


def first_fix_kernel(
    came, first_t, held, node_op, vec_op, corner, smoothed, fix, back, full, behind, work
):
    def first_core():
        behind[...] = smoothed[:B]
        subtract(first_t[...], came[:B], held, work)
        fix_all(work, node_op, vec_op, corner, fix, back, full)

    pl.when(jnp.logical_not(is_second()))(first_core)


def second_fix_kernel(
    came, couplings, last_t, held, node_op, vec_op, corner, full_first, fix, full, swap, work
):
    def first_core():
        swap[: 2 * B] = full_first[...]

    def second_core():
        subtract(last_t[...], dot3(couplings[3], came[...]), held, work)
        fix_all(work, node_op, vec_op, corner, fix, swap, full)

    by_core(first_core, second_core)


def base_kernel(smoothed, fix_first, fix_second, wide_first, wide_second, came, column, out):
    def first_core():
        mats = came[2 * B :]
        folded = jnp.concatenate([unpack(mats[:, : 2 * B]), unpack(mats[:, 2 * B :])], axis=0)
        partial = came[: 2 * B] - dot3(folded, smoothed[:B])
        blocks = jnp.concatenate([*here(wide_first), column[...]], axis=1)
        out[...] = smoothed[...] + dot3(blocks, jnp.concatenate([fix_first[...], partial], axis=0))

    def second_core():
        out[...] = smoothed[...] + dot3(jnp.concatenate(here(wide_second), axis=1), fix_second[...])

    by_core(first_core, second_core)


def here(wide):
    return [wide[0], wide[1], wide[2], wide[NODE]]


def next_fix(came, full):
    corner = came[2 * B : 2 * B + 64]
    vec = came[:B] + dot3(unpack(corner[:, : 2 * B]), full[:B])
    node = came[B : 2 * B] + dot3(unpack(corner[:, 2 * B :]), full[B:])
    return [vec, node]


def next_term(came, full, wide):
    blocks = jnp.concatenate([wide[V_NEXT], wide[N_NEXT]], axis=1)
    return dot3(blocks, jnp.concatenate(next_fix(came, full), axis=0))


def first_end_kernel(came, full, wide, column, base, out, more, work, sem):
    def first_core():
        work[...] = base[...] + next_term(came, full, wide)
        copy = pltpu.make_async_copy(work, out, sem)
        copy.start()
        copy.wait()

    def second_core():
        more[...] = base[...] + dot3(column[...], came[: 2 * B])

    by_core(first_core, second_core)


def second_end_kernel(came, full, wide, more, _, out, work, sem):
    def second_core():
        work[...] = more[...] + next_term(came, full, wide)
        copy = pltpu.make_async_copy(work, out, sem)
        copy.start()
        copy.wait()

    pl.when(is_second())(second_core)


VMEM = pl.BlockSpec(memory_space=pltpu.VMEM)
HBM = pl.BlockSpec(memory_space=pltpu.HBM)
ANY = pl.BlockSpec(memory_space=pl.ANY)

PATTERNS = [pltpu.SMEM((2, 4), jnp.int32), pltpu.SMEM((2, 4), jnp.int32), pltpu.SemaphoreType.DMA((2,))]


def call(kernel, outs, in_specs, *args, scratch=(), units=0, out_specs=None, aliases=None):
    return pl.pallas_call(
        kernel,
        out_shape=[jax.ShapeDtypeStruct(shape, dtype) for shape, dtype in outs],
        in_specs=in_specs,
        out_specs=out_specs or [VMEM] * len(outs),
        input_output_aliases=aliases or {},
        scratch_shapes=list(scratch),
        compiler_params=pltpu.CompilerParams(vmem_limit_bytes=24 * 1024 * 1024),
        cost_estimate=pl.CostEstimate(flops=units * 50331648, bytes_accessed=units, transcendentals=0),
    )(*args)


def local(
    right_side,
    smoother,
    diagonal_blocks,
    couplings,
    grad_blocks,
    grad_pattern,
    interp_blocks,
    interp_pattern,
    node_smoother,
    vector_smoother,
    node_aggregates,
    vector_aggregates,
    node_coarse,
    vector_coarse,
):
    vectors = right_side.shape[1]
    pats = (grad_pattern.T, interp_pattern.T)

    swap, ahead, behind = chip_pairs()

    fetched_here = (diagonal_blocks, grad_blocks, interp_blocks)
    sent_ahead, sent_swap, diagonal, grad_blocks, interp_blocks = call(
        send_kernel,
        [((B + 8, vectors), F32), ((B, vectors), F32), *((x.shape, F32) for x in fetched_here)],
        [HBM] * 6,
        *(pltpu.with_memory_space_constraint(x, pltpu.HBM) for x in (right_side, smoother, couplings, *fetched_here)),
        scratch=[
            pltpu.VMEM((B, vectors), F32),
            pltpu.VMEM((B, vectors), F32),
            pltpu.VMEM((3, B, B), F32),
            pltpu.SemaphoreType.DMA((8,)),
        ],
    )
    came_ahead = crossed(sent_ahead, ahead)
    came_swap = crossed(sent_swap, swap)

    smoothed, resid, named_next, folded = call(
        resid_kernel,
        [((4 * B, vectors), F32), ((4 * B, vectors), F32), ((2 * B, 12 * B), BF16), ((64, vectors), F32)],
        [VMEM] * 8,
        *pats, right_side, smoother, diagonal, couplings, grad_blocks, interp_blocks,
        scratch=[pltpu.VMEM((4 * B, 2 * B), F32)],
        units=0,
    )
    (partial,) = call(
        partial_kernel,
        [((2 * B + 64, vectors), F32)],
        [VMEM] * 4,
        came_swap, resid, named_next, folded,
        units=0,
    )
    came_partial = crossed(partial, ahead)

    mats = (node_smoother, vector_smoother, node_aggregates, vector_aggregates, node_coarse, vector_coarse, grad_blocks, interp_blocks)
    prepared = [
        ((B, 3 * B), BF16),
        ((3 * B, 9 * B), BF16),
        ((64, vectors), F32),
        ((SLOTS, 4 * B, B), F32),
        ((4 * B, 2 * B), F32),
        ((SLOTS, B, vectors), F32),
        ((SLOTS * B, 3 * B), BF16),
    ]
    sizes = [((4 * B, vectors), F32), ((2 * B + 64, vectors), F32), ((2 * B, vectors), F32), ((B, vectors), F32)]
    longer = ((2 * B + 72, vectors), F32)
    work = pltpu.VMEM((SLOTS, B, vectors), F32)
    node_op, vec_op, corner, wide_first, column_first, held, first_t = call(
        first_prepare_kernel,
        prepared,
        [ANY] * 2 + [VMEM] * 11 + [ANY],
        *pats, *mats, resid, came_swap, couplings, partial,
        scratch=PATTERNS,
        units=0,
    )
    fix_first, sent_back, full_first, sent_behind = call(
        first_fix_kernel,
        [sizes[0], longer, *sizes[2:]],
        [VMEM] * 7,
        came_ahead, first_t, held, node_op, vec_op, corner, smoothed,
        scratch=[work],
        units=0,
    )
    came_behind = crossed(sent_behind, behind)
    came_back = crossed(sent_back, behind)
    node_op, vec_op, corner, wide_second, column_second, held, last_t = call(
        second_prepare_kernel,
        prepared,
        [ANY] * 2 + [VMEM] * 11 + [ANY],
        *pats, *mats, resid, came_swap, couplings, sent_back,
        scratch=PATTERNS,
        units=100,
    )
    fix_second, full_second, sent_swap = call(
        second_fix_kernel,
        [sizes[0], sizes[2], sizes[1]],
        [VMEM] * 8,
        came_behind, couplings, last_t, held, node_op, vec_op, corner, full_first,
        scratch=[work],
        units=0,
    )
    came_swap = crossed(sent_swap, swap)
    (base,) = call(
        base_kernel,
        [((4 * B, vectors), F32)],
        [VMEM] * 7,
        smoothed, fix_first, fix_second, wide_first, wide_second, came_partial, column_first,
        units=60,
    )
    work = [pltpu.VMEM((4 * B, vectors), F32), pltpu.SemaphoreType.DMA]
    out, more = call(
        first_end_kernel,
        [((4 * B, vectors), F32)] * 2,
        [VMEM] * 5,
        came_swap, full_first, wide_first, column_second, base,
        scratch=work,
        out_specs=[ANY, VMEM],
        units=0,
    )
    (out,) = call(
        second_end_kernel,
        [((4 * B, vectors), F32)],
        [VMEM] * 4 + [ANY],
        came_back, full_second, wide_second, more, out,
        scratch=work,
        out_specs=[ANY],
        aliases={4: 0},
    )
    return out


def solution(mesh):
    in_specs = (
        P("region", None),
        P("region", None, None),
        P("region", None, None),
        P("region", None, None),
        P("region", None, None, None),
        P("region", None),
        P("region", None, None, None),
        P("region", None),
        P("region", None, None),
        P("region", None, None),
        P("region"),
        P("region"),
        P("region", None),
        P("region", None),
    )
    out_specs = P("region", None)
    return jax.shard_map(local, mesh=mesh, in_specs=in_specs, out_specs=out_specs, check_vma=False)
```

```python
import jax
import jax.numpy as jnp
from jax import lax
from jax.experimental import pallas as pl
from jax.experimental.pallas import tpu as pltpu
from jax.sharding import PartitionSpec as P

F32 = jnp.float32
BF16 = jnp.bfloat16
B = 128
SLOTS = 6
V_NEXT, NODE, N_NEXT = 3, 4, 5


def crossed(x, pairs):
    return lax.ppermute(x, "region", pairs)


def chip_pairs():
    size = lax.axis_size("region")
    swap = [(i, i ^ 1) for i in range(size)]
    ahead = [(i, i + 1) for i in range(1, size - 1, 2)]
    return swap, ahead, [(b, a) for a, b in ahead]


def is_second():
    return lax.axis_index("region") % 2 == 1


def by_core(first, second):
    pl.when(jnp.logical_not(is_second()))(first)
    pl.when(is_second())(second)


def split(x):
    high = x.astype(BF16)
    return high, (x - high.astype(F32)).astype(BF16)


def left(x):
    high, low = split(x)
    return jnp.concatenate([high, high, low], axis=1)


def right(x):
    high, low = split(x)
    return jnp.concatenate([high, low, high], axis=0)


def mul(x, y):
    return jnp.dot(x, y, preferred_element_type=F32)


def dot3(x, y):
    return mul(left(x), right(y))


def pack(x):
    return jnp.concatenate([x[:64], x[64:]], axis=1)


def unpack(x):
    return jnp.concatenate([x[:, :B], x[:, B:]], axis=0)


def transposed(blocks):
    return left(jnp.concatenate([x.T for x in blocks], axis=0))


def slots_of(gpat, ipat, k):
    return [NODE + gpat[0, k], NODE + gpat[1, k], ipat[0, k], ipat[1, k]]


def fetched(gfrom, ifrom, gpat, ipat, sems):
    copies = [pltpu.make_async_copy(gfrom, gpat, sems.at[0]), pltpu.make_async_copy(ifrom, ipat, sems.at[1])]
    for copy in copies:
        copy.start()
    return copies


def wait_all(copies):
    for copy in copies:
        copy.wait()


def named(pattern, s, k, block, value):
    return jnp.where(pattern[s : s + 1, k : k + 1] == value, block, 0.0)


def send_kernel(
    source, smoother, couplings, diagonal_from, grad_from, interp_from, ahead, swap, diagonal, grad, interp, last, first, mats, sems
):
    moves = [
        (source.at[pl.ds(3 * B, B)], last),
        (smoother.at[3], mats.at[0]),
        (couplings.at[3], mats.at[1]),
        (source.at[pl.ds(0, B)], first),
        (smoother.at[0], mats.at[2]),
        (diagonal_from, diagonal),
        (grad_from, grad),
        (interp_from, interp),
    ]
    copies = [pltpu.make_async_copy(a, b, sems.at[i]) for i, (a, b) in enumerate(moves)]
    for copy in copies:
        copy.start()
    wait_all(copies[:5])
    smoothed = dot3(mats[0], last[...])
    beside = dot3(mats[2], first[...])
    onward = dot3(mats[1].T, smoothed)
    ahead[:B] = onward
    swap[...] = jnp.where(is_second(), beside, onward)
    wait_all(copies[5:])


def resid_kernel(gpat, ipat, source, smoother, diagonal, couplings, grad, interp, smoothed, resid, first_next, local_next, folded, total):
    for k in range(4):
        smoothed[k * B : (k + 1) * B] = dot3(smoother[k], source[k * B : (k + 1) * B])
        rows = slice(k * B, (k + 1) * B)
        total[rows, :B] = sum(named(ipat, s, k, interp[k, s], 3) for s in range(2))
        total[rows, B:] = sum(named(gpat, s, k, grad[k, s], 1) for s in range(2))
    next_t = total[...].T
    first_next[...] = left(next_t[:, :B])
    mats = dot3(next_t[:, 3 * B :], couplings[3])
    folded[:, : 2 * B] = pack(mats[:B])
    folded[:, 2 * B :] = pack(mats[B:])
    zero = jnp.zeros((B, B), F32)
    high, low = split(smoothed[...])
    for half in range(2):
        rows = []
        for k in (2 * half, 2 * half + 1):
            row = [zero] * 3
            row[k - half] = diagonal[k]
            if k:
                row[k - half - 1] = couplings[k - 1].T if k - half else row[k - half - 1]
            if k - half < 2:
                row[k - half + 1] = couplings[k]
            rows.append(jnp.concatenate(row, axis=1))
        here = slice(half * B, (half + 3) * B)
        got = jnp.concatenate([high[here], low[here], high[here]], axis=0)
        at = slice(2 * half * B, 2 * (half + 1) * B)
        resid[at] = source[at] - mul(left(jnp.concatenate(rows, axis=0)), got)
    local_next[...] = mul(left(next_t), right(resid[...]))


def partial_kernel(came, first_next, local_next, folded, partial):
    def second_core():
        partial[: 2 * B] = local_next[...] - mul(first_next[...], right(came[...]))
        partial[2 * B :] = folded[...]

    pl.when(is_second())(second_core)


def subtract(blocks, x, held, work):
    terms = mul(blocks, right(x))
    for slot in range(SLOTS):
        work[slot] = held[slot] - terms[slot * B : (slot + 1) * B]


def operators(gpat, ipat, nsm, vsm, nagg, vagg, ncoarse, vcoarse, grad, interp, node_op, vec_op, corner, wide, column):
    def folded(aggregates, coarse):
        width = aggregates.shape[0]
        onehot = (lax.broadcasted_iota(jnp.int32, (B, width), 0) == aggregates[...][None, :]).astype(F32)
        high, low = split(coarse[...])
        pick = onehot.astype(BF16)
        cols = mul(jnp.concatenate([high, low], axis=1), jnp.concatenate([pick, pick], axis=0))
        back = onehot.T.astype(BF16)
        high, low = split(cols)
        return mul(jnp.concatenate([back, back], axis=1), jnp.concatenate([high, low], axis=0))

    n_op = nsm[0] + folded(nagg, ncoarse)
    node_op[...] = left(n_op)
    v_op = folded(vagg, vcoarse)
    zero = jnp.zeros((B, B), F32)
    v_op = v_op + jnp.concatenate(
        [jnp.concatenate([vsm[i] if i == j else zero for j in range(3)], axis=1) for i in range(3)], axis=0
    )
    vec_op[...] = left(v_op)
    corner[:, : 2 * B] = pack(v_op[:B, :B])
    corner[:, 2 * B :] = pack(n_op)
    wide[...] = jnp.zeros_like(wide)
    for k in range(4):
        slots = slots_of(gpat, ipat, k)
        blocks = [grad[k, 0], grad[k, 1], interp[k, 0], interp[k, 1]]
        for slot, block in zip(slots, blocks):
            wide[slot, k * B : (k + 1) * B] += block
    vec = jnp.concatenate([wide[0], wide[1], wide[2]], axis=1)
    column[:, :B] = dot3(vec, v_op[:, :B])
    column[:, B:] = dot3(wide[NODE], n_op)


def fix_all(work, node_op, vec_op, corner, fix, back, full):
    vec = mul(vec_op[...], right(jnp.concatenate([work[0], work[1], work[2]], axis=0)))
    node = mul(node_op[...], right(work[NODE]))
    fix[: 3 * B] = vec
    fix[3 * B :] = node
    back[:B] = vec[:B]
    back[B : 2 * B] = node
    back[2 * B : 2 * B + 64] = corner[...]
    full[:B] = work[V_NEXT]
    full[B:] = work[N_NEXT]


def prepare(keep, gfrom, ifrom, *refs):
    mats, (resid, came, couplings), outs = refs[:8], refs[8:11], refs[12:]
    node_op, vec_op, corner, wide, column, held, kept, gpat, ipat, sems = outs
    grad, interp = mats[6:]
    wait_all(fetched(gfrom, ifrom, gpat, ipat, sems))
    operators(gpat, ipat, *mats, node_op, vec_op, corner, wide, column)
    kept[...] = transposed([wide[slot, keep * B : (keep + 1) * B] for slot in range(SLOTS)])
    held[...] = jnp.zeros_like(held)
    for k in range(4):
        blocks = transposed([grad[k, 0], grad[k, 1], interp[k, 0], interp[k, 1]])
        rows = resid[k * B : (k + 1) * B]
        if keep == 0 and k == 3:
            rows = rows - dot3(couplings[3], came[...])
        if keep == 3 and k == 0:
            rows = rows - came[...]
        terms = mul(blocks, right(rows))
        for i, slot in enumerate(slots_of(gpat, ipat, k)):
            held[slot] += terms[i * B : (i + 1) * B]


def first_prepare_kernel(*refs):
    pl.when(jnp.logical_not(is_second()))(lambda: prepare(0, *refs))


def second_prepare_kernel(*refs):
    pl.when(is_second())(lambda: prepare(3, *refs))


def first_fix_kernel(
    came, first_t, held, node_op, vec_op, corner, smoothed, fix, back, full, behind, work
):
    def first_core():
        behind[...] = smoothed[:B]
        subtract(first_t[...], came[:B], held, work)
        fix_all(work, node_op, vec_op, corner, fix, back, full)

    pl.when(jnp.logical_not(is_second()))(first_core)


def second_fix_kernel(
    came, couplings, last_t, held, node_op, vec_op, corner, full_first, fix, full, swap, work
):
    def first_core():
        swap[: 2 * B] = full_first[...]

    def second_core():
        subtract(last_t[...], dot3(couplings[3], came[...]), held, work)
        fix_all(work, node_op, vec_op, corner, fix, swap, full)

    by_core(first_core, second_core)


def base_kernel(smoothed, fix_first, fix_second, wide_first, wide_second, came, column, out):
    def first_core():
        mats = came[2 * B :]
        folded = jnp.concatenate([unpack(mats[:, : 2 * B]), unpack(mats[:, 2 * B :])], axis=0)
        partial = came[: 2 * B] - dot3(folded, smoothed[:B])
        blocks = jnp.concatenate([*here(wide_first), column[...]], axis=1)
        out[...] = smoothed[...] + dot3(blocks, jnp.concatenate([fix_first[...], partial], axis=0))

    def second_core():
        out[...] = smoothed[...] + dot3(jnp.concatenate(here(wide_second), axis=1), fix_second[...])

    by_core(first_core, second_core)


def here(wide):
    return [wide[0], wide[1], wide[2], wide[NODE]]


def next_fix(came, full):
    corner = came[2 * B : 2 * B + 64]
    vec = came[:B] + dot3(unpack(corner[:, : 2 * B]), full[:B])
    node = came[B : 2 * B] + dot3(unpack(corner[:, 2 * B :]), full[B:])
    return [vec, node]


def next_term(came, full, wide):
    blocks = jnp.concatenate([wide[V_NEXT], wide[N_NEXT]], axis=1)
    return dot3(blocks, jnp.concatenate(next_fix(came, full), axis=0))


def first_end_kernel(came, full, wide, column, base, out, more, work, sem):
    def first_core():
        work[...] = base[...] + next_term(came, full, wide)
        copy = pltpu.make_async_copy(work, out, sem)
        copy.start()
        copy.wait()

    def second_core():
        more[...] = base[...] + dot3(column[...], came[: 2 * B])

    by_core(first_core, second_core)


def second_end_kernel(came, full, wide, more, _, out, work, sem):
    def second_core():
        work[...] = more[...] + next_term(came, full, wide)
        copy = pltpu.make_async_copy(work, out, sem)
        copy.start()
        copy.wait()

    pl.when(is_second())(second_core)


VMEM = pl.BlockSpec(memory_space=pltpu.VMEM)
HBM = pl.BlockSpec(memory_space=pltpu.HBM)
ANY = pl.BlockSpec(memory_space=pl.ANY)

PATTERNS = [pltpu.SMEM((2, 4), jnp.int32), pltpu.SMEM((2, 4), jnp.int32), pltpu.SemaphoreType.DMA((2,))]


def call(kernel, outs, in_specs, *args, scratch=(), units=0, out_specs=None, aliases=None):
    return pl.pallas_call(
        kernel,
        out_shape=[jax.ShapeDtypeStruct(shape, dtype) for shape, dtype in outs],
        in_specs=in_specs,
        out_specs=out_specs or [VMEM] * len(outs),
        input_output_aliases=aliases or {},
        scratch_shapes=list(scratch),
        compiler_params=pltpu.CompilerParams(vmem_limit_bytes=24 * 1024 * 1024),
        cost_estimate=pl.CostEstimate(flops=units * 50331648, bytes_accessed=units, transcendentals=0),
    )(*args)


def local(
    right_side,
    smoother,
    diagonal_blocks,
    couplings,
    grad_blocks,
    grad_pattern,
    interp_blocks,
    interp_pattern,
    node_smoother,
    vector_smoother,
    node_aggregates,
    vector_aggregates,
    node_coarse,
    vector_coarse,
):
    vectors = right_side.shape[1]
    pats = (grad_pattern.T, interp_pattern.T)

    swap, ahead, behind = chip_pairs()

    fetched_here = (diagonal_blocks, grad_blocks, interp_blocks)
    sent_ahead, sent_swap, diagonal, grad_blocks, interp_blocks = call(
        send_kernel,
        [((B + 8, vectors), F32), ((B, vectors), F32), *((x.shape, F32) for x in fetched_here)],
        [HBM] * 6,
        *(pltpu.with_memory_space_constraint(x, pltpu.HBM) for x in (right_side, smoother, couplings, *fetched_here)),
        scratch=[
            pltpu.VMEM((B, vectors), F32),
            pltpu.VMEM((B, vectors), F32),
            pltpu.VMEM((3, B, B), F32),
            pltpu.SemaphoreType.DMA((8,)),
        ],
    )
    came_ahead = crossed(sent_ahead, ahead)
    came_swap = crossed(sent_swap, swap)

    smoothed, resid, first_next, local_next, folded = call(
        resid_kernel,
        [((4 * B, vectors), F32), ((4 * B, vectors), F32), ((2 * B, 3 * B), BF16), ((2 * B, vectors), F32), ((64, vectors), F32)],
        [VMEM] * 8,
        *pats, right_side, smoother, diagonal, couplings, grad_blocks, interp_blocks,
        scratch=[pltpu.VMEM((4 * B, 2 * B), F32)],
        units=0,
    )
    (partial,) = call(
        partial_kernel,
        [((2 * B + 64, vectors), F32)],
        [VMEM] * 4,
        came_swap, first_next, local_next, folded,
        units=0,
    )
    came_partial = crossed(partial, ahead)

    mats = (node_smoother, vector_smoother, node_aggregates, vector_aggregates, node_coarse, vector_coarse, grad_blocks, interp_blocks)
    prepared = [
        ((B, 3 * B), BF16),
        ((3 * B, 9 * B), BF16),
        ((64, vectors), F32),
        ((SLOTS, 4 * B, B), F32),
        ((4 * B, 2 * B), F32),
        ((SLOTS, B, vectors), F32),
        ((SLOTS * B, 3 * B), BF16),
    ]
    sizes = [((4 * B, vectors), F32), ((2 * B + 64, vectors), F32), ((2 * B, vectors), F32), ((B, vectors), F32)]
    longer = ((2 * B + 72, vectors), F32)
    work = pltpu.VMEM((SLOTS, B, vectors), F32)
    node_op, vec_op, corner, wide_first, column_first, held, first_t = call(
        first_prepare_kernel,
        prepared,
        [ANY] * 2 + [VMEM] * 11 + [ANY],
        *pats, *mats, resid, came_swap, couplings, partial,
        scratch=PATTERNS,
        units=0,
    )
    fix_first, sent_back, full_first, sent_behind = call(
        first_fix_kernel,
        [sizes[0], longer, *sizes[2:]],
        [VMEM] * 7,
        came_ahead, first_t, held, node_op, vec_op, corner, smoothed,
        scratch=[work],
        units=0,
    )
    came_behind = crossed(sent_behind, behind)
    came_back = crossed(sent_back, behind)
    node_op, vec_op, corner, wide_second, column_second, held, last_t = call(
        second_prepare_kernel,
        prepared,
        [ANY] * 2 + [VMEM] * 11 + [ANY],
        *pats, *mats, resid, came_swap, couplings, sent_back,
        scratch=PATTERNS,
        units=100,
    )
    fix_second, full_second, sent_swap = call(
        second_fix_kernel,
        [sizes[0], sizes[2], sizes[1]],
        [VMEM] * 8,
        came_behind, couplings, last_t, held, node_op, vec_op, corner, full_first,
        scratch=[work],
        units=0,
    )
    came_swap = crossed(sent_swap, swap)
    (base,) = call(
        base_kernel,
        [((4 * B, vectors), F32)],
        [VMEM] * 7,
        smoothed, fix_first, fix_second, wide_first, wide_second, came_partial, column_first,
        units=60,
    )
    work = [pltpu.VMEM((4 * B, vectors), F32), pltpu.SemaphoreType.DMA]
    out, more = call(
        first_end_kernel,
        [((4 * B, vectors), F32)] * 2,
        [VMEM] * 5,
        came_swap, full_first, wide_first, column_second, base,
        scratch=work,
        out_specs=[ANY, VMEM],
        units=0,
    )
    (out,) = call(
        second_end_kernel,
        [((4 * B, vectors), F32)],
        [VMEM] * 4 + [ANY],
        came_back, full_second, wide_second, more, out,
        scratch=work,
        out_specs=[ANY],
        aliases={4: 0},
    )
    return out


def solution(mesh):
    in_specs = (
        P("region", None),
        P("region", None, None),
        P("region", None, None),
        P("region", None, None),
        P("region", None, None, None),
        P("region", None),
        P("region", None, None, None),
        P("region", None),
        P("region", None, None),
        P("region", None, None),
        P("region"),
        P("region"),
        P("region", None),
        P("region", None),
    )
    out_specs = P("region", None)
    return jax.shard_map(local, mesh=mesh, in_specs=in_specs, out_specs=out_specs, check_vma=False)
```
